32 devices in a mesh: groups: 2 (over y), row: 4 (over z), col: 4 (over x, core).
Axes of the slice: x: 2, y: 2, z: 4, core: 2. Of those that a mesh axis runs over, the one named last changes fastest.
Arguments:
- pair_act: bfloat16 [64, 32, 128], P(('groups', 'row'), 'col'), parts along dimension 0, may hold values from -6 to 6
- cotangent: bfloat16 [64, 32, 128], P(('groups', 'row'), 'col'), parts along dimension 0, may hold values from -6 to 6
- crop_len: int32 [2], P('groups'), parts along dimension 0, may hold values from 16 to 32
- ln_in_gain: float32 [128], replicated, may hold values from 0.5 to 1.5
- ln_in_bias: float32 [128], replicated, may hold values from -3 to 3
- w_left: bfloat16 [128, 256], replicated, may hold values from -0.5 to 0.5
- w_right: bfloat16 [128, 256], replicated, may hold values from -0.5 to 0.5
- w_gate: bfloat16 [128, 128], replicated, may hold values from -0.5 to 0.5
- ln_out_gain: float32 [128], replicated, may hold values from 0.5 to 1.5
- ln_out_bias: float32 [128], replicated, may hold values from -3 to 3
- w_out: bfloat16 [128, 128], replicated, may hold values from -0.5 to 0.5
Outputs:
- d_pair: bfloat16 [64, 32, 128], P(('groups', 'row'), 'col'), parts along dimension 0
The draws below stay inside these ranges and needn't reach their ends.
There are 2 independent parts, one for each index of `groups`. The reference program is written for one: setup_inputs(seed, part) draws one part's arguments, and reference() takes and returns one part's arrays. A program takes and returns all parts, laid end to end along the dimension named above; an argument that names none is the same for every part. Nothing has to cross between parts.
All inputs are finite; a program needn't handle non-finite values.
Results may differ from the reference program's by a relative error of at most 0.014.
Values may be sent and summed in bfloat16 or wider, within the bound.
A program may use at most 64 MiB of HBM per device.

```python
import jax
import jax.numpy as jnp
from jax import lax

CHANNELS = 128
HIDDEN_SIZE = 128
CROP = 32
N_ROW = 4


def block_levels(key, extent, shards, smallest, high):
    level = 1.0
    for position, parts in shards:
        steps = jax.random.uniform(jax.random.fold_in(jax.random.fold_in(key, 6), position), (parts,), jnp.float32, smallest / len(shards), high / len(shards))
        level = level * jnp.repeat(jnp.exp(steps), extent[position] // parts).reshape((-1,) + (1,) * (len(extent) - 1 - position))
    return level


def centred(key, extent, width, most, cuts=(), held_as=jnp.bfloat16):
    gain = block_levels(key, extent, cuts, -0.22, 0.18) if cuts else 1.0
    drawn = jax.random.normal(key, extent, jnp.float32) * width * gain
    return jnp.minimum(jnp.maximum(drawn, -most), most).astype(held_as)


def setup_inputs(seed: int = 0, part: int = 0) -> dict:
    arg_keys = jax.random.split(jax.random.key(seed), 12)
    part_keys = jax.random.split(jax.random.fold_in(arg_keys[11], part), 12)
    pair_act = centred(part_keys[0], (CROP, CROP, CHANNELS), 1.0, 6.0, ((0, 4), (1, 4)))
    cotangent = centred(part_keys[1], (CROP, CROP, CHANNELS), 1.0, 6.0, ((0, 4), (1, 4)))
    crop_len = jax.random.randint(part_keys[2], (1,), CROP // 2, CROP + 1).astype(jnp.int32)
    ln_in_gain = jnp.clip(jax.random.uniform(arg_keys[3], (CHANNELS,), jnp.float32, 0.5, 1.5), 0.5, 1.5)
    ln_in_bias = centred(arg_keys[4], (CHANNELS,), 0.5, 3.0, (), jnp.float32)
    w_left = centred(arg_keys[5], (CHANNELS, 2 * HIDDEN_SIZE), CHANNELS ** -0.5, 0.5)
    w_right = centred(arg_keys[6], (CHANNELS, 2 * HIDDEN_SIZE), CHANNELS ** -0.5, 0.5)
    w_gate = centred(arg_keys[7], (CHANNELS, CHANNELS), CHANNELS ** -0.5, 0.5)
    ln_out_gain = jnp.clip(jax.random.uniform(arg_keys[8], (HIDDEN_SIZE,), jnp.float32, 0.5, 1.5), 0.5, 1.5)
    ln_out_bias = centred(arg_keys[9], (HIDDEN_SIZE,), 0.5, 3.0, (), jnp.float32)
    w_out = centred(arg_keys[10], (HIDDEN_SIZE, CHANNELS), HIDDEN_SIZE ** -0.5, 0.5)
    return dict(pair_act=pair_act, cotangent=cotangent, crop_len=crop_len, ln_in_gain=ln_in_gain, ln_in_bias=ln_in_bias, w_left=w_left, w_right=w_right, w_gate=w_gate, ln_out_gain=ln_out_gain, ln_out_bias=ln_out_bias, w_out=w_out)


epsilon = 1e-05

def normalize(values):
    center = lax.optimization_barrier(jnp.mean(values, axis=-1, keepdims=True))
    shifted = values - center
    inv_std = lax.rsqrt(lax.optimization_barrier(jnp.mean(shifted * shifted, axis=-1, keepdims=True)) + epsilon)
    return (shifted * inv_std, inv_std)

def norm_back(d_scaled, scaled, inv_std):
    first = lax.optimization_barrier(jnp.mean(d_scaled, axis=-1, keepdims=True))
    second = lax.optimization_barrier(jnp.mean(d_scaled * scaled, axis=-1, keepdims=True))
    return inv_std * (d_scaled - first - scaled * second)

def gated_proj(projected, pair_mask, hidden_width):
    linear = projected[..., :hidden_width]
    sigmoid_part = jax.nn.sigmoid(projected[..., hidden_width:])
    return (linear, sigmoid_part, pair_mask * sigmoid_part * linear)

def reference(pair_act, cotangent, crop_len, ln_in_gain, ln_in_bias, w_left, w_right, w_gate, ln_out_gain, ln_out_bias, w_out):
    crop_size = pair_act.shape[0]
    hidden_width = w_out.shape[0]
    positions = jnp.arange(crop_size, dtype=jnp.int32)
    valid = (positions < crop_len[0]).astype(jnp.float32)
    pair_mask = valid[:, None, None] * valid[None, :, None]
    hat_in, inv_in = normalize(pair_act.astype(jnp.float32))
    normed = (hat_in * ln_in_gain + ln_in_bias).astype(jnp.bfloat16)
    left_lin, left_sig, left_full = gated_proj(jnp.dot(normed, w_left, preferred_element_type=jnp.float32), pair_mask, hidden_width)
    left_side = left_full.astype(jnp.bfloat16)
    right_lin, right_sig, right_full = gated_proj(jnp.dot(normed, w_right, preferred_element_type=jnp.float32), pair_mask, hidden_width)
    right_side = right_full.astype(jnp.bfloat16)
    gating = jax.nn.sigmoid(jnp.dot(normed, w_gate, preferred_element_type=jnp.float32))
    update = jnp.einsum('ikh,jkh->ijh', left_side.astype(jnp.float32), right_side.astype(jnp.float32), precision=lax.Precision.HIGHEST)
    hat_out, inv_out = normalize(update)
    mixed = (hat_out * ln_out_gain + ln_out_bias).astype(jnp.bfloat16)
    proj_out = jnp.dot(mixed, w_out, preferred_element_type=jnp.float32)
    cot_full = cotangent.astype(jnp.float32)
    d_proj = (cot_full * gating).astype(jnp.bfloat16)
    d_gate_pre = cot_full * proj_out * gating * (1.0 - gating)
    d_mixed = jnp.dot(d_proj, w_out.T, preferred_element_type=jnp.float32)
    d_update = norm_back(d_mixed * ln_out_gain, hat_out, inv_out).astype(jnp.bfloat16)
    d_left = jnp.einsum('ijh,jkh->ikh', d_update.astype(jnp.float32), right_side.astype(jnp.float32), precision=lax.Precision.HIGHEST)
    block_rows = crop_size // N_ROW
    update_blocks = d_update.reshape(N_ROW, block_rows, crop_size, hidden_width)
    left_blocks = left_side.reshape(N_ROW, block_rows, crop_size, hidden_width)

    def add_block(running, pieces):
        grad_block, left_block = pieces
        partial_sum = jnp.einsum('ijh,ikh->jkh', grad_block.astype(jnp.float32), left_block.astype(jnp.float32), precision=lax.Precision.HIGHEST)
        rounded = lax.optimization_barrier(partial_sum.astype(jnp.bfloat16))
        return (running + rounded.astype(jnp.float32), None)
    d_right, _ = lax.scan(add_block, jnp.zeros((crop_size, crop_size, hidden_width), jnp.float32), (update_blocks, left_blocks))
    d_pre = jnp.concatenate([d_left * pair_mask * left_sig, d_left * pair_mask * left_lin * left_sig * (1.0 - left_sig), d_right * pair_mask * right_sig, d_right * pair_mask * right_lin * right_sig * (1.0 - right_sig), d_gate_pre], axis=-1).astype(jnp.bfloat16)
    w_joined = jnp.concatenate([w_left, w_right, w_gate], axis=1)
    d_normed = jnp.dot(d_pre, w_joined.T, preferred_element_type=jnp.float32)
    return norm_back(d_normed * ln_in_gain, hat_in, inv_in).astype(jnp.bfloat16)
```

```python
import functools

import jax
import jax.numpy as jnp
from jax import lax
from jax.experimental import pallas as pl
from jax.experimental.pallas import tpu as pltpu
from jax.sharding import PartitionSpec as P

epsilon = 1e-05
MESH = pl.DeviceIdType.MESH


def normalize(values):
    center = jnp.mean(values, axis=-1, keepdims=True)
    shifted = values - center
    inv_std = lax.rsqrt(jnp.mean(shifted * shifted, axis=-1, keepdims=True) + epsilon)
    return (shifted * inv_std, inv_std)


def norm_back(d_scaled, scaled, inv_std):
    first = jnp.mean(d_scaled, axis=-1, keepdims=True)
    second = jnp.mean(d_scaled * scaled, axis=-1, keepdims=True)
    return inv_std * (d_scaled - first - scaled * second)


def dot(a, b):
    return jnp.dot(a, b, preferred_element_type=jnp.float32)


def dot_t(a, b):
    return lax.dot_general(a, b, (((1,), (1,)), ((), ())), preferred_element_type=jnp.float32)


def loop(count, body, init):
    if count <= 4:
        for step in range(count):
            init = body(step, init)
        return init
    return lax.fori_loop(0, count, body, init)


def each(start, count, body):
    if count <= 16:
        for step in range(start, count):
            body(step)
    else:

        @pl.loop(start, count)
        def _(step):
            body(step)


def kernel(
    n_row,
    n_col,
    rows,
    cols,
    crop_ref,
    pair_ref,
    cot_ref,
    gain_in_ref,
    bias_in_ref,
    w_left_ref,
    w_right_ref,
    w_gate_ref,
    gain_out_ref,
    bias_out_ref,
    w_out_ref,
    out_ref,
    left_own,
    right_own,
    turn_own,
    grad_own,
    left_row,
    right_turn,
    left_panel,
    right_panel,
    grad_row,
    grad_col,
    right_wide,
    left_wide,
    grad_row_wide,
    grad_col_wide,
    left_row_out,
    left_row_in,
    turn_out,
    turn_in,
    left_panel_out,
    left_panel_in,
    right_panel_out,
    right_panel_in,
    grad_row_out,
    grad_row_in,
    grad_col_out,
    grad_col_in,
):
    row = lax.axis_index("row")
    col = lax.axis_index("col")
    ratio = cols // rows
    cells = rows * cols
    sub = rows * rows
    width = w_out_ref.shape[0]
    home_col = row // ratio
    total = n_row * n_col

    barrier = pltpu.get_barrier_semaphore()

    def greet(step):
        other = lax.rem(row * n_col + col + step, total)
        pl.semaphore_signal(
            barrier,
            inc=1,
            device_id={"row": other // n_col, "col": lax.rem(other, n_col)},
            device_id_type=MESH,
        )

    each(1, total, greet)

    def remote(src, dst, out_sem, in_sem, to_row, to_col):
        return pltpu.make_async_remote_copy(
            src_ref=src,
            dst_ref=dst,
            send_sem=out_sem,
            recv_sem=in_sem,
            device_id={"row": to_row, "col": to_col},
            device_id_type=MESH,
        )

    position = (rows, cols, width)
    row_pos = row * rows + lax.broadcasted_iota(jnp.int32, position, 0)
    col_pos = col * cols + lax.broadcasted_iota(jnp.int32, position, 1)
    crop = crop_ref[0]
    pair_mask = jnp.where(jnp.maximum(row_pos, col_pos) < crop, 1.0, 0.0).reshape(cells, width)
    hat_in, inv_in = normalize(pair_ref[...].astype(jnp.float32))
    gain_in = gain_in_ref[...]
    normed = (hat_in * gain_in + bias_in_ref[...]).astype(jnp.bfloat16)
    right_proj = dot(normed, w_right_ref[...])
    right_lin = right_proj[:, :width]
    right_sig = jax.nn.sigmoid(right_proj[:, width:])
    right_side = (pair_mask * right_sig * right_lin).astype(jnp.bfloat16)
    right_own[...] = right_side
    right_wide[...] = right_side.astype(jnp.float32)
    turn_own[...] = jnp.concatenate(
        [right_wide[pl.ds(k, rows, stride=cols), :] for k in range(cols)], axis=0
    ).astype(jnp.bfloat16)
    left_proj = dot(normed, w_left_ref[...])
    left_lin = left_proj[:, :width]
    left_sig = jax.nn.sigmoid(left_proj[:, width:])
    left_own[...] = (pair_mask * left_sig * left_lin).astype(jnp.bfloat16)

    pl.semaphore_wait(barrier, total - 1)

    turn_slot = lax.rem(row, ratio) * n_col + col

    def turn_copy(step):
        return remote(
            turn_own,
            right_turn.at[turn_slot],
            turn_out.at[step],
            turn_in.at[turn_slot],
            lax.rem(row + step, n_row),
            home_col,
        )

    each(1, n_row, lambda step: turn_copy(step).start())

    @pl.when(home_col != col)
    def _():
        turn_copy(0).start()

    @pl.when(home_col == col)
    def _():
        pltpu.make_async_copy(turn_own, right_turn.at[turn_slot], turn_in.at[turn_slot]).start()

    def left_row_copy(step):
        return remote(
            left_own,
            left_row.at[col],
            left_row_out.at[step],
            left_row_in.at[col],
            row,
            lax.rem(col + step, n_col),
        )

    each(1, n_col, lambda step: left_row_copy(step).start())

    def right_panel_copy(step):
        return remote(
            right_own,
            right_panel.at[row],
            right_panel_out.at[step],
            right_panel_in.at[row],
            lax.rem(row + step, n_row),
            col,
        )

    def left_panel_copy(step):
        return remote(
            left_own,
            left_panel.at[row],
            left_panel_out.at[step],
            left_panel_in.at[row],
            lax.rem(row + step, n_row),
            col,
        )

    each(1, n_row, lambda step: right_panel_copy(step).start())
    each(1, n_row, lambda step: left_panel_copy(step).start())

    left_row[col] = left_own[...]
    right_panel[row] = right_own[...]
    left_panel[row] = left_own[...]

    gating = jax.nn.sigmoid(dot(normed, w_gate_ref[...]))
    cot_full = cot_ref[...].astype(jnp.float32)
    d_proj = (cot_full * gating).astype(jnp.bfloat16)
    gain_out = gain_out_ref[...]
    d_scaled = dot_t(d_proj, w_out_ref[...]) * gain_out

    def arrived(buffer, sem, slot):
        remote(buffer.at[slot], buffer.at[slot], sem.at[slot], sem.at[slot], row, col).wait_recv()

    each(1, n_col, lambda step: arrived(left_row, left_row_in, lax.rem(col + step, n_col)))
    each(0, ratio * n_col, lambda slot: arrived(right_turn, turn_in, slot))

    left_wide[...] = left_row[...].astype(jnp.float32)

    def add_update(source, sums):
        sums = list(sums)
        for part in range(ratio):
            turned = right_turn[part * n_col + source].astype(jnp.float32)
            for k in range(cols):
                turned_k = turned[k * rows : (k + 1) * rows]
                for i in range(rows):
                    at = part * rows + i
                    sums[at] += left_wide[source, i * cols + k : i * cols + k + 1, :] * turned_k
        return tuple(sums)

    zero = jnp.zeros((rows, width), jnp.float32)
    sums = loop(n_col, add_update, (zero,) * (ratio * rows))
    update = jnp.concatenate(
        [sums[part * rows + i] for i in range(rows) for part in range(ratio)], axis=0
    )
    hat_out, inv_out = normalize(update)
    d_update = norm_back(d_scaled, hat_out, inv_out)
    for part in range(ratio):
        grad_own[part] = jnp.concatenate(
            [
                d_update[i * cols + part * rows : i * cols + (part + 1) * rows]
                for i in range(rows)
            ],
            axis=0,
        ).astype(jnp.bfloat16)

    def grad_col_copy(part, to_col):
        return remote(
            grad_own.at[part],
            grad_col.at[row],
            grad_col_out.at[part * n_col + to_col],
            grad_col_in.at[row],
            col * ratio + part,
            to_col,
        )

    for part in range(ratio):

        def send_part(to_col, part=part):
            own = jnp.logical_and(col * ratio + part == row, to_col == col)

            @pl.when(jnp.logical_not(own))
            def _():
                grad_col_copy(part, to_col).start()

            @pl.when(own)
            def _():
                pltpu.make_async_copy(
                    grad_own.at[part], grad_col.at[row], grad_col_in.at[row]
                ).start()

        each(0, n_col, send_part)

    def grad_row_copy(step):
        slots = pl.ds(col * ratio, ratio)
        return remote(
            grad_own,
            grad_row.at[slots],
            grad_row_out.at[step],
            grad_row_in.at[col],
            row,
            lax.rem(col + step, n_col),
        )

    each(1, n_col, lambda step: grad_row_copy(step).start())
    grad_row[pl.ds(col * ratio, ratio)] = grad_own[...]

    mixed = (hat_out * gain_out + bias_out_ref[...]).astype(jnp.bfloat16)
    proj_out = dot(mixed, w_out_ref[...])
    d_gate_pre = (cot_full * proj_out * gating * (1.0 - gating)).astype(jnp.bfloat16)
    d_normed = dot_t(d_gate_pre, w_gate_ref[...])
    each(1, n_row, lambda step: arrived(right_panel, right_panel_in, lax.rem(row + step, n_row)))
    each(1, n_row, lambda step: arrived(left_panel, left_panel_in, lax.rem(row + step, n_row)))

    def grad_row_arrived(step):
        source = lax.rem(col + step, n_col)
        slots = pl.ds(source * ratio, ratio)
        remote(
            grad_row.at[slots],
            grad_row.at[slots],
            grad_row_in.at[source],
            grad_row_in.at[source],
            row,
            col,
        ).wait_recv()

    each(1, n_col, grad_row_arrived)
    grad_row_wide[...] = grad_row[...].astype(jnp.float32)

    def add_left(source, sums):
        sums = list(sums)
        panel = right_panel[source].astype(jnp.float32)
        for j in range(rows):
            panel_j = panel[j * cols : (j + 1) * cols]
            for i in range(rows):
                sums[i] += grad_row_wide[source, i * rows + j : i * rows + j + 1, :] * panel_j
        return tuple(sums)

    zero_wide = jnp.zeros((cols, width), jnp.float32)
    d_left = jnp.concatenate(loop(n_row, add_left, (zero_wide,) * rows), axis=0)
    left_part = d_left * pair_mask * left_sig
    d_left_pre = jnp.concatenate([left_part, left_part * left_lin * (1.0 - left_sig)], axis=1)
    d_normed += dot_t(d_left_pre.astype(jnp.bfloat16), w_left_ref[...])

    each(0, n_row, lambda slot: arrived(grad_col, grad_col_in, slot))
    grad_col_wide[...] = grad_col[...].astype(jnp.float32)

    def add_right(source, sums):
        sums = list(sums)
        panel = left_panel[source].astype(jnp.float32)
        for i in range(rows):
            panel_i = panel[i * cols : (i + 1) * cols]
            for j in range(rows):
                sums[j] += grad_col_wide[source, i * rows + j : i * rows + j + 1, :] * panel_i
        return tuple(sums)

    d_right = jnp.concatenate(loop(n_row, add_right, (zero_wide,) * rows), axis=0)
    right_part = d_right * pair_mask * right_sig
    d_right_pre = jnp.concatenate([right_part, right_part * right_lin * (1.0 - right_sig)], axis=1)
    d_normed += dot_t(d_right_pre.astype(jnp.bfloat16), w_right_ref[...])
    out_ref[...] = norm_back(d_normed * gain_in, hat_in, inv_in).astype(jnp.bfloat16)

    each(1, n_row, lambda step: turn_copy(step).wait_send())

    @pl.when(home_col != col)
    def _():
        turn_copy(0).wait_send()

    each(1, n_col, lambda step: left_row_copy(step).wait_send())
    each(1, n_row, lambda step: right_panel_copy(step).wait_send())
    each(1, n_row, lambda step: left_panel_copy(step).wait_send())
    each(1, n_col, lambda step: grad_row_copy(step).wait_send())
    for part in range(ratio):

        def sent_part(to_col, part=part):
            own = jnp.logical_and(col * ratio + part == row, to_col == col)

            @pl.when(jnp.logical_not(own))
            def _():
                grad_col_copy(part, to_col).wait_send()

        each(0, n_col, sent_part)


def solution(mesh):
    n_row = mesh.shape["row"]
    n_col = mesh.shape["col"]

    def shards(
        pair_act,
        cotangent,
        crop_len,
        ln_in_gain,
        ln_in_bias,
        w_left,
        w_right,
        w_gate,
        ln_out_gain,
        ln_out_bias,
        w_out,
    ):
        rows, cols, channels = pair_act.shape
        width = w_out.shape[0]
        ratio = cols // rows
        assert ratio * rows == cols and n_row * rows == n_col * cols
        cells, sub = rows * cols, rows * rows
        vmem = pl.BlockSpec(memory_space=pltpu.VMEM)
        half, full, sems = jnp.bfloat16, jnp.float32, pltpu.SemaphoreType.DMA
        result = pl.pallas_call(
            functools.partial(kernel, n_row, n_col, rows, cols),
            out_shape=jax.ShapeDtypeStruct((cells, channels), half),
            in_specs=[pl.BlockSpec(memory_space=pltpu.SMEM)] + [vmem] * 10,
            out_specs=vmem,
            scratch_shapes=[
                pltpu.VMEM((cells, width), half),
                pltpu.VMEM((cells, width), half),
                pltpu.VMEM((cells, width), half),
                pltpu.VMEM((ratio, sub, width), half),
                pltpu.VMEM((n_col, cells, width), half),
                pltpu.VMEM((ratio * n_col, cells, width), half),
                pltpu.VMEM((n_row, cells, width), half),
                pltpu.VMEM((n_row, cells, width), half),
                pltpu.VMEM((n_row, sub, width), half),
                pltpu.VMEM((n_row, sub, width), half),
                pltpu.VMEM((cells, width), full),
                pltpu.VMEM((n_col, cells, width), full),
                pltpu.VMEM((n_row, sub, width), full),
                pltpu.VMEM((n_row, sub, width), full),
                sems((n_col,)),
                sems((n_col,)),
                sems((n_row,)),
                sems((ratio * n_col,)),
                sems((n_row,)),
                sems((n_row,)),
                sems((n_row,)),
                sems((n_row,)),
                sems((n_col,)),
                sems((n_col,)),
                sems((ratio * n_col,)),
                sems((n_row,)),
            ],
            compiler_params=pltpu.CompilerParams(
                collective_id=0, has_side_effects=True, vmem_limit_bytes=32 * 1024 * 1024
            ),
        )(
            crop_len,
            pair_act.reshape(cells, channels),
            cotangent.reshape(cells, channels),
            ln_in_gain.reshape(1, channels),
            ln_in_bias.reshape(1, channels),
            w_left,
            w_right,
            w_gate,
            ln_out_gain.reshape(1, width),
            ln_out_bias.reshape(1, width),
            w_out,
        )
        return result.reshape(rows, cols, channels)

    pair_spec = P(("groups", "row"), "col", None)
    return jax.shard_map(
        shards,
        mesh=mesh,
        in_specs=(pair_spec, pair_spec, P("groups")) + (P(),) * 8,
        out_specs=pair_spec,
        check_vma=False,
    )
```

```python
import functools

import jax
import jax.numpy as jnp
from jax import lax
from jax.experimental import pallas as pl
from jax.experimental.pallas import tpu as pltpu
from jax.sharding import PartitionSpec as P

epsilon = 1e-05
MESH = pl.DeviceIdType.MESH


def normalize(values):
    center = jnp.mean(values, axis=-1, keepdims=True)
    shifted = values - center
    inv_std = lax.rsqrt(jnp.mean(shifted * shifted, axis=-1, keepdims=True) + epsilon)
    return (shifted * inv_std, inv_std)


def norm_back(d_scaled, scaled, inv_std):
    first = jnp.mean(d_scaled, axis=-1, keepdims=True)
    second = jnp.mean(d_scaled * scaled, axis=-1, keepdims=True)
    return inv_std * (d_scaled - first - scaled * second)


def dot(a, b):
    return jnp.dot(a, b, preferred_element_type=jnp.float32)


def dot_t(a, b):
    return lax.dot_general(a, b, (((1,), (1,)), ((), ())), preferred_element_type=jnp.float32)


def loop(count, body, init):
    if count <= 4:
        for step in range(count):
            init = body(step, init)
        return init
    return lax.fori_loop(0, count, body, init)


def each(start, count, body):
    if count <= 16:
        for step in range(start, count):
            body(step)
    else:

        @pl.loop(start, count)
        def _(step):
            body(step)


def kernel(
    n_row,
    n_col,
    rows,
    cols,
    crop_hbm,
    pair_hbm,
    cot_hbm,
    gain_in_hbm,
    bias_in_hbm,
    w_left_hbm,
    w_right_hbm,
    w_gate_hbm,
    gain_out_hbm,
    bias_out_hbm,
    w_out_hbm,
    out_ref,
    crop_ref,
    pair_ref,
    cot_ref,
    gain_in_ref,
    bias_in_ref,
    w_left_ref,
    w_right_ref,
    w_gate_ref,
    gain_out_ref,
    bias_out_ref,
    w_out_ref,
    load_in,
    left_own,
    right_own,
    turn_own,
    grad_own,
    left_row,
    right_turn,
    left_panel,
    right_panel,
    grad_row,
    grad_col,
    right_wide,
    left_wide,
    grad_row_wide,
    grad_col_wide,
    left_row_out,
    left_row_in,
    turn_out,
    turn_in,
    left_panel_out,
    left_panel_in,
    right_panel_out,
    right_panel_in,
    grad_row_out,
    grad_row_in,
    grad_col_out,
    grad_col_in,
):
    row = lax.axis_index("row")
    col = lax.axis_index("col")
    ratio = cols // rows
    cells = rows * cols
    sub = rows * rows
    width = w_out_ref.shape[0]
    home_col = row // ratio
    total = n_row * n_col

    barrier = pltpu.get_barrier_semaphore()

    def greet(step):
        other = lax.rem(row * n_col + col + step, total)
        pl.semaphore_signal(
            barrier,
            inc=1,
            device_id={"row": other // n_col, "col": lax.rem(other, n_col)},
            device_id_type=MESH,
        )

    each(1, total, greet)

    pairs = (
        (pair_hbm, pair_ref),
        (gain_in_hbm, gain_in_ref),
        (bias_in_hbm, bias_in_ref),
        (w_right_hbm, w_right_ref),
        (w_left_hbm, w_left_ref),
        (crop_hbm, crop_ref),
        (w_gate_hbm, w_gate_ref),
        (cot_hbm, cot_ref),
        (w_out_hbm, w_out_ref),
        (gain_out_hbm, gain_out_ref),
        (bias_out_hbm, bias_out_ref),
    )
    loads = [pltpu.make_async_copy(*pair, load_in.at[at]) for at, pair in enumerate(pairs)]
    for load in loads:
        load.start()

    def remote(src, dst, out_sem, in_sem, to_row, to_col):
        return pltpu.make_async_remote_copy(
            src_ref=src,
            dst_ref=dst,
            send_sem=out_sem,
            recv_sem=in_sem,
            device_id={"row": to_row, "col": to_col},
            device_id_type=MESH,
        )

    for load in loads[:6]:
        load.wait()
    position = (rows, cols, width)
    row_pos = row * rows + lax.broadcasted_iota(jnp.int32, position, 0)
    col_pos = col * cols + lax.broadcasted_iota(jnp.int32, position, 1)
    crop = crop_ref[0]
    pair_mask = jnp.where(jnp.maximum(row_pos, col_pos) < crop, 1.0, 0.0).reshape(cells, width)
    hat_in, inv_in = normalize(pair_ref[...].astype(jnp.float32))
    gain_in = gain_in_ref[...]
    normed = (hat_in * gain_in + bias_in_ref[...]).astype(jnp.bfloat16)
    right_proj = dot(normed, w_right_ref[...])
    right_lin = right_proj[:, :width]
    right_sig = jax.nn.sigmoid(right_proj[:, width:])
    right_side = (pair_mask * right_sig * right_lin).astype(jnp.bfloat16)
    right_own[...] = right_side
    right_wide[...] = right_side.astype(jnp.float32)
    turn_own[...] = jnp.concatenate(
        [right_wide[pl.ds(k, rows, stride=cols), :] for k in range(cols)], axis=0
    ).astype(jnp.bfloat16)
    left_proj = dot(normed, w_left_ref[...])
    left_lin = left_proj[:, :width]
    left_sig = jax.nn.sigmoid(left_proj[:, width:])
    left_own[...] = (pair_mask * left_sig * left_lin).astype(jnp.bfloat16)

    pl.semaphore_wait(barrier, total - 1)

    turn_slot = lax.rem(row, ratio) * n_col + col

    def turn_copy(step):
        return remote(
            turn_own,
            right_turn.at[turn_slot],
            turn_out.at[step],
            turn_in.at[turn_slot],
            lax.rem(row + step, n_row),
            home_col,
        )

    each(1, n_row, lambda step: turn_copy(step).start())

    @pl.when(home_col != col)
    def _():
        turn_copy(0).start()

    @pl.when(home_col == col)
    def _():
        pltpu.make_async_copy(turn_own, right_turn.at[turn_slot], turn_in.at[turn_slot]).start()

    def left_row_copy(step):
        return remote(
            left_own,
            left_row.at[col],
            left_row_out.at[step],
            left_row_in.at[col],
            row,
            lax.rem(col + step, n_col),
        )

    each(1, n_col, lambda step: left_row_copy(step).start())

    def right_panel_copy(step):
        return remote(
            right_own,
            right_panel.at[row],
            right_panel_out.at[step],
            right_panel_in.at[row],
            lax.rem(row + step, n_row),
            col,
        )

    def left_panel_copy(step):
        return remote(
            left_own,
            left_panel.at[row],
            left_panel_out.at[step],
            left_panel_in.at[row],
            lax.rem(row + step, n_row),
            col,
        )

    each(1, n_row, lambda step: right_panel_copy(step).start())
    each(1, n_row, lambda step: left_panel_copy(step).start())

    left_row[col] = left_own[...]
    right_panel[row] = right_own[...]
    left_panel[row] = left_own[...]

    for load in loads[6:]:
        load.wait()
    gating = jax.nn.sigmoid(dot(normed, w_gate_ref[...]))
    cot_full = cot_ref[...].astype(jnp.float32)
    d_proj = (cot_full * gating).astype(jnp.bfloat16)
    gain_out = gain_out_ref[...]
    d_scaled = dot_t(d_proj, w_out_ref[...]) * gain_out

    def arrived(buffer, sem, slot):
        remote(buffer.at[slot], buffer.at[slot], sem.at[slot], sem.at[slot], row, col).wait_recv()

    each(1, n_col, lambda step: arrived(left_row, left_row_in, lax.rem(col + step, n_col)))
    each(0, ratio * n_col, lambda slot: arrived(right_turn, turn_in, slot))

    left_wide[...] = left_row[...].astype(jnp.float32)

    def add_update(source, sums):
        sums = list(sums)
        for part in range(ratio):
            turned = right_turn[part * n_col + source].astype(jnp.float32)
            for k in range(cols):
                turned_k = turned[k * rows : (k + 1) * rows]
                for i in range(rows):
                    at = part * rows + i
                    sums[at] += left_wide[source, i * cols + k : i * cols + k + 1, :] * turned_k
        return tuple(sums)

    zero = jnp.zeros((rows, width), jnp.float32)
    sums = loop(n_col, add_update, (zero,) * (ratio * rows))
    update = jnp.concatenate(
        [sums[part * rows + i] for i in range(rows) for part in range(ratio)], axis=0
    )
    hat_out, inv_out = normalize(update)
    d_update = norm_back(d_scaled, hat_out, inv_out)
    for part in range(ratio):
        grad_own[part] = jnp.concatenate(
            [
                d_update[i * cols + part * rows : i * cols + (part + 1) * rows]
                for i in range(rows)
            ],
            axis=0,
        ).astype(jnp.bfloat16)

    def grad_col_copy(part, to_col):
        return remote(
            grad_own.at[part],
            grad_col.at[row],
            grad_col_out.at[part * n_col + to_col],
            grad_col_in.at[row],
            col * ratio + part,
            to_col,
        )

    for part in range(ratio):

        def send_part(to_col, part=part):
            own = jnp.logical_and(col * ratio + part == row, to_col == col)

            @pl.when(jnp.logical_not(own))
            def _():
                grad_col_copy(part, to_col).start()

            @pl.when(own)
            def _():
                pltpu.make_async_copy(
                    grad_own.at[part], grad_col.at[row], grad_col_in.at[row]
                ).start()

        each(0, n_col, send_part)

    def grad_row_copy(step):
        slots = pl.ds(col * ratio, ratio)
        return remote(
            grad_own,
            grad_row.at[slots],
            grad_row_out.at[step],
            grad_row_in.at[col],
            row,
            lax.rem(col + step, n_col),
        )

    each(1, n_col, lambda step: grad_row_copy(step).start())
    grad_row[pl.ds(col * ratio, ratio)] = grad_own[...]

    mixed = (hat_out * gain_out + bias_out_ref[...]).astype(jnp.bfloat16)
    proj_out = dot(mixed, w_out_ref[...])
    d_gate_pre = (cot_full * proj_out * gating * (1.0 - gating)).astype(jnp.bfloat16)
    d_normed = dot_t(d_gate_pre, w_gate_ref[...])
    each(1, n_row, lambda step: arrived(right_panel, right_panel_in, lax.rem(row + step, n_row)))
    each(1, n_row, lambda step: arrived(left_panel, left_panel_in, lax.rem(row + step, n_row)))

    def grad_row_arrived(step):
        source = lax.rem(col + step, n_col)
        slots = pl.ds(source * ratio, ratio)
        remote(
            grad_row.at[slots],
            grad_row.at[slots],
            grad_row_in.at[source],
            grad_row_in.at[source],
            row,
            col,
        ).wait_recv()

    each(1, n_col, grad_row_arrived)
    grad_row_wide[...] = grad_row[...].astype(jnp.float32)

    def add_left(source, sums):
        sums = list(sums)
        panel = right_panel[source].astype(jnp.float32)
        for j in range(rows):
            panel_j = panel[j * cols : (j + 1) * cols]
            for i in range(rows):
                sums[i] += grad_row_wide[source, i * rows + j : i * rows + j + 1, :] * panel_j
        return tuple(sums)

    zero_wide = jnp.zeros((cols, width), jnp.float32)
    d_left = jnp.concatenate(loop(n_row, add_left, (zero_wide,) * rows), axis=0)
    left_part = d_left * pair_mask * left_sig
    d_left_pre = jnp.concatenate([left_part, left_part * left_lin * (1.0 - left_sig)], axis=1)
    d_normed += dot_t(d_left_pre.astype(jnp.bfloat16), w_left_ref[...])

    each(0, n_row, lambda slot: arrived(grad_col, grad_col_in, slot))
    grad_col_wide[...] = grad_col[...].astype(jnp.float32)

    def add_right(source, sums):
        sums = list(sums)
        panel = left_panel[source].astype(jnp.float32)
        for i in range(rows):
            panel_i = panel[i * cols : (i + 1) * cols]
            for j in range(rows):
                sums[j] += grad_col_wide[source, i * rows + j : i * rows + j + 1, :] * panel_i
        return tuple(sums)

    d_right = jnp.concatenate(loop(n_row, add_right, (zero_wide,) * rows), axis=0)
    right_part = d_right * pair_mask * right_sig
    d_right_pre = jnp.concatenate([right_part, right_part * right_lin * (1.0 - right_sig)], axis=1)
    d_normed += dot_t(d_right_pre.astype(jnp.bfloat16), w_right_ref[...])
    out_ref[...] = norm_back(d_normed * gain_in, hat_in, inv_in).astype(jnp.bfloat16)

    each(1, n_row, lambda step: turn_copy(step).wait_send())

    @pl.when(home_col != col)
    def _():
        turn_copy(0).wait_send()

    each(1, n_col, lambda step: left_row_copy(step).wait_send())
    each(1, n_row, lambda step: right_panel_copy(step).wait_send())
    each(1, n_row, lambda step: left_panel_copy(step).wait_send())
    each(1, n_col, lambda step: grad_row_copy(step).wait_send())
    for part in range(ratio):

        def sent_part(to_col, part=part):
            own = jnp.logical_and(col * ratio + part == row, to_col == col)

            @pl.when(jnp.logical_not(own))
            def _():
                grad_col_copy(part, to_col).wait_send()

        each(0, n_col, sent_part)


def solution(mesh):
    n_row = mesh.shape["row"]
    n_col = mesh.shape["col"]

    def shards(
        pair_act,
        cotangent,
        crop_len,
        ln_in_gain,
        ln_in_bias,
        w_left,
        w_right,
        w_gate,
        ln_out_gain,
        ln_out_bias,
        w_out,
    ):
        rows, cols, channels = pair_act.shape
        width = w_out.shape[0]
        ratio = cols // rows
        assert ratio * rows == cols and n_row * rows == n_col * cols
        cells, sub = rows * cols, rows * rows
        half, full, sems = jnp.bfloat16, jnp.float32, pltpu.SemaphoreType.DMA
        result = pl.pallas_call(
            functools.partial(kernel, n_row, n_col, rows, cols),
            out_shape=jax.ShapeDtypeStruct((cells, channels), half),
            in_specs=[pl.BlockSpec(memory_space=pltpu.HBM)] * 11,
            out_specs=pl.BlockSpec(memory_space=pltpu.VMEM),
            scratch_shapes=[
                pltpu.SMEM(crop_len.shape, jnp.int32),
                pltpu.VMEM((cells, channels), half),
                pltpu.VMEM((cells, channels), half),
                pltpu.VMEM((1, channels), full),
                pltpu.VMEM((1, channels), full),
                pltpu.VMEM(w_left.shape, half),
                pltpu.VMEM(w_right.shape, half),
                pltpu.VMEM(w_gate.shape, half),
                pltpu.VMEM((1, width), full),
                pltpu.VMEM((1, width), full),
                pltpu.VMEM(w_out.shape, half),
                sems((11,)),
                pltpu.VMEM((cells, width), half),
                pltpu.VMEM((cells, width), half),
                pltpu.VMEM((cells, width), half),
                pltpu.VMEM((ratio, sub, width), half),
                pltpu.VMEM((n_col, cells, width), half),
                pltpu.VMEM((ratio * n_col, cells, width), half),
                pltpu.VMEM((n_row, cells, width), half),
                pltpu.VMEM((n_row, cells, width), half),
                pltpu.VMEM((n_row, sub, width), half),
                pltpu.VMEM((n_row, sub, width), half),
                pltpu.VMEM((cells, width), full),
                pltpu.VMEM((n_col, cells, width), full),
                pltpu.VMEM((n_row, sub, width), full),
                pltpu.VMEM((n_row, sub, width), full),
                sems((n_col,)),
                sems((n_col,)),
                sems((n_row,)),
                sems((ratio * n_col,)),
                sems((n_row,)),
                sems((n_row,)),
                sems((n_row,)),
                sems((n_row,)),
                sems((n_col,)),
                sems((n_col,)),
                sems((ratio * n_col,)),
                sems((n_row,)),
            ],
            compiler_params=pltpu.CompilerParams(
                collective_id=0, has_side_effects=True, vmem_limit_bytes=60 * 1024 * 1024
            ),
        )(
            crop_len,
            pair_act.reshape(cells, channels),
            cotangent.reshape(cells, channels),
            ln_in_gain.reshape(1, channels),
            ln_in_bias.reshape(1, channels),
            w_left,
            w_right,
            w_gate,
            ln_out_gain.reshape(1, width),
            ln_out_bias.reshape(1, width),
            w_out,
        )
        return result.reshape(rows, cols, channels)

    pair_spec = P(("groups", "row"), "col", None)
    return jax.shard_map(
        shards,
        mesh=mesh,
        in_specs=(pair_spec, pair_spec, P("groups")) + (P(),) * 8,
        out_specs=pair_spec,
        check_vma=False,
    )
```

```python
import functools

import jax
import jax.numpy as jnp
from jax import lax
from jax.experimental import pallas as pl
from jax.experimental.pallas import tpu as pltpu
from jax.sharding import PartitionSpec as P

epsilon = 1e-05
MESH = pl.DeviceIdType.MESH


def normalize(values):
    center = jnp.mean(values, axis=-1, keepdims=True)
    shifted = values - center
    inv_std = lax.rsqrt(jnp.mean(shifted * shifted, axis=-1, keepdims=True) + epsilon)
    return (shifted * inv_std, inv_std)


def norm_back(d_scaled, scaled, inv_std):
    first = jnp.mean(d_scaled, axis=-1, keepdims=True)
    second = jnp.mean(d_scaled * scaled, axis=-1, keepdims=True)
    return inv_std * (d_scaled - first - scaled * second)


def dot(a, b):
    return jnp.dot(a, b, preferred_element_type=jnp.float32)


def dot_t(a, b):
    return lax.dot_general(a, b, (((1,), (1,)), ((), ())), preferred_element_type=jnp.float32)


def loop(count, body, init):
    if count <= 4:
        for step in range(count):
            init = body(step, init)
        return init
    return lax.fori_loop(0, count, body, init)


def each(start, count, body):
    if count <= 16:
        for step in range(start, count):
            body(step)
    else:

        @pl.loop(start, count)
        def _(step):
            body(step)


def kernel(
    n_row,
    n_col,
    rows,
    cols,
    crop_hbm,
    pair_hbm,
    cot_hbm,
    gain_in_hbm,
    bias_in_hbm,
    w_left_hbm,
    w_right_hbm,
    w_gate_hbm,
    gain_out_hbm,
    bias_out_hbm,
    w_out_hbm,
    out_ref,
    crop_ref,
    pair_ref,
    cot_ref,
    gain_in_ref,
    bias_in_ref,
    w_left_ref,
    w_right_ref,
    w_gate_ref,
    gain_out_ref,
    bias_out_ref,
    w_out_ref,
    load_in,
    side_own,
    turn_own,
    grad_own,
    left_row,
    right_turn,
    panel,
    grad_row,
    grad_col,
    right_wide,
    left_wide,
    grad_row_wide,
    grad_col_wide,
    left_row_out,
    left_row_in,
    turn_out,
    turn_in,
    panel_out,
    panel_in,
    grad_row_out,
    grad_row_in,
    grad_col_out,
    grad_col_in,
):
    row = lax.axis_index("row")
    col = lax.axis_index("col")
    ratio = cols // rows
    cells = rows * cols
    sub = rows * rows
    width = w_out_ref.shape[0]
    home_col = row // ratio
    total = n_row * n_col

    barrier = pltpu.get_barrier_semaphore()

    def greet(step):
        other = lax.rem(row * n_col + col + step, total)
        pl.semaphore_signal(
            barrier,
            inc=1,
            device_id={"row": other // n_col, "col": lax.rem(other, n_col)},
            device_id_type=MESH,
        )

    each(1, total, greet)

    pairs = (
        (pair_hbm, pair_ref),
        (gain_in_hbm, gain_in_ref),
        (bias_in_hbm, bias_in_ref),
        (w_right_hbm, w_right_ref),
        (w_left_hbm, w_left_ref),
        (crop_hbm, crop_ref),
        (w_gate_hbm, w_gate_ref),
        (cot_hbm, cot_ref),
        (w_out_hbm, w_out_ref),
        (gain_out_hbm, gain_out_ref),
        (bias_out_hbm, bias_out_ref),
    )
    loads = [pltpu.make_async_copy(*pair, load_in.at[at]) for at, pair in enumerate(pairs)]
    for load in loads:
        load.start()

    def remote(src, dst, out_sem, in_sem, to_row, to_col):
        return pltpu.make_async_remote_copy(
            src_ref=src,
            dst_ref=dst,
            send_sem=out_sem,
            recv_sem=in_sem,
            device_id={"row": to_row, "col": to_col},
            device_id_type=MESH,
        )

    for load in loads[:6]:
        load.wait()
    position = (rows, cols, width)
    row_pos = row * rows + lax.broadcasted_iota(jnp.int32, position, 0)
    col_pos = col * cols + lax.broadcasted_iota(jnp.int32, position, 1)
    crop = crop_ref[0]
    pair_mask = jnp.where(jnp.maximum(row_pos, col_pos) < crop, 1.0, 0.0).reshape(cells, width)
    hat_in, inv_in = normalize(pair_ref[...].astype(jnp.float32))
    gain_in = gain_in_ref[...]
    normed = (hat_in * gain_in + bias_in_ref[...]).astype(jnp.bfloat16)
    right_proj = dot(normed, w_right_ref[...])
    right_lin = right_proj[:, :width]
    right_sig = jax.nn.sigmoid(right_proj[:, width:])
    right_side = (pair_mask * right_sig * right_lin).astype(jnp.bfloat16)
    side_own[1] = right_side
    right_wide[...] = right_side.astype(jnp.float32)
    turn_own[...] = jnp.concatenate(
        [right_wide[pl.ds(k, rows, stride=cols), :] for k in range(cols)], axis=0
    ).astype(jnp.bfloat16)

    pl.semaphore_wait(barrier, total - 1)

    turn_slot = lax.rem(row, ratio) * n_col + col

    def turn_copy(step):
        return remote(
            turn_own,
            right_turn.at[turn_slot],
            turn_out.at[step],
            turn_in.at[turn_slot],
            lax.rem(row + step, n_row),
            home_col,
        )

    each(1, n_row, lambda step: turn_copy(step).start())

    @pl.when(home_col != col)
    def _():
        turn_copy(0).start()

    @pl.when(home_col == col)
    def _():
        pltpu.make_async_copy(turn_own, right_turn.at[turn_slot], turn_in.at[turn_slot]).start()

    left_proj = dot(normed, w_left_ref[...])
    left_lin = left_proj[:, :width]
    left_sig = jax.nn.sigmoid(left_proj[:, width:])
    side_own[0] = (pair_mask * left_sig * left_lin).astype(jnp.bfloat16)

    def left_row_copy(step):
        return remote(
            side_own.at[0],
            left_row.at[col],
            left_row_out.at[step],
            left_row_in.at[col],
            row,
            lax.rem(col + step, n_col),
        )

    each(1, n_col, lambda step: left_row_copy(step).start())

    def panel_copy(step):
        return remote(
            side_own,
            panel.at[row],
            panel_out.at[step],
            panel_in.at[row],
            lax.rem(row + step, n_row),
            col,
        )

    each(1, n_row, lambda step: panel_copy(step).start())

    left_row[col] = side_own[0]
    panel[row] = side_own[...]

    for load in loads[6:]:
        load.wait()
    gating = jax.nn.sigmoid(dot(normed, w_gate_ref[...]))
    cot_full = cot_ref[...].astype(jnp.float32)
    d_proj = (cot_full * gating).astype(jnp.bfloat16)
    gain_out = gain_out_ref[...]
    d_scaled = dot_t(d_proj, w_out_ref[...]) * gain_out

    def arrived(buffer, sem, slot):
        remote(buffer.at[slot], buffer.at[slot], sem.at[slot], sem.at[slot], row, col).wait_recv()

    each(1, n_col, lambda step: arrived(left_row, left_row_in, lax.rem(col + step, n_col)))
    each(0, ratio * n_col, lambda slot: arrived(right_turn, turn_in, slot))

    left_wide[...] = left_row[...].astype(jnp.float32)

    def add_update(source, sums):
        sums = list(sums)
        for part in range(ratio):
            turned = right_turn[part * n_col + source].astype(jnp.float32)
            for k in range(cols):
                turned_k = turned[k * rows : (k + 1) * rows]
                for i in range(rows):
                    at = part * rows + i
                    sums[at] += left_wide[source, i * cols + k : i * cols + k + 1, :] * turned_k
        return tuple(sums)

    zero = jnp.zeros((rows, width), jnp.float32)
    sums = loop(n_col, add_update, (zero,) * (ratio * rows))
    update = jnp.concatenate(
        [sums[part * rows + i] for i in range(rows) for part in range(ratio)], axis=0
    )
    hat_out, inv_out = normalize(update)
    d_update = norm_back(d_scaled, hat_out, inv_out)
    for part in range(ratio):
        grad_own[part] = jnp.concatenate(
            [
                d_update[i * cols + part * rows : i * cols + (part + 1) * rows]
                for i in range(rows)
            ],
            axis=0,
        ).astype(jnp.bfloat16)

    def grad_col_copy(part, to_col):
        return remote(
            grad_own.at[part],
            grad_col.at[row],
            grad_col_out.at[part * n_col + to_col],
            grad_col_in.at[row],
            col * ratio + part,
            to_col,
        )

    for part in range(ratio):

        def send_part(to_col, part=part):
            own = jnp.logical_and(col * ratio + part == row, to_col == col)

            @pl.when(jnp.logical_not(own))
            def _():
                grad_col_copy(part, to_col).start()

            @pl.when(own)
            def _():
                pltpu.make_async_copy(
                    grad_own.at[part], grad_col.at[row], grad_col_in.at[row]
                ).start()

        each(0, n_col, send_part)

    def grad_row_copy(step):
        slots = pl.ds(col * ratio, ratio)
        return remote(
            grad_own,
            grad_row.at[slots],
            grad_row_out.at[step],
            grad_row_in.at[col],
            row,
            lax.rem(col + step, n_col),
        )

    each(1, n_col, lambda step: grad_row_copy(step).start())
    grad_row[pl.ds(col * ratio, ratio)] = grad_own[...]

    mixed = (hat_out * gain_out + bias_out_ref[...]).astype(jnp.bfloat16)
    proj_out = dot(mixed, w_out_ref[...])
    d_gate_pre = (cot_full * proj_out * gating * (1.0 - gating)).astype(jnp.bfloat16)
    d_normed = dot_t(d_gate_pre, w_gate_ref[...])
    each(1, n_row, lambda step: arrived(panel, panel_in, lax.rem(row + step, n_row)))

    def grad_row_arrived(step):
        source = lax.rem(col + step, n_col)
        slots = pl.ds(source * ratio, ratio)
        remote(
            grad_row.at[slots],
            grad_row.at[slots],
            grad_row_in.at[source],
            grad_row_in.at[source],
            row,
            col,
        ).wait_recv()

    each(1, n_col, grad_row_arrived)
    grad_row_wide[...] = grad_row[...].astype(jnp.float32)

    def add_left(source, sums):
        sums = list(sums)
        right = panel[source, 1].astype(jnp.float32)
        for j in range(rows):
            right_j = right[j * cols : (j + 1) * cols]
            for i in range(rows):
                sums[i] += grad_row_wide[source, i * rows + j : i * rows + j + 1, :] * right_j
        return tuple(sums)

    zero_wide = jnp.zeros((cols, width), jnp.float32)
    d_left = jnp.concatenate(loop(n_row, add_left, (zero_wide,) * rows), axis=0)
    left_part = d_left * pair_mask * left_sig
    d_left_pre = jnp.concatenate([left_part, left_part * left_lin * (1.0 - left_sig)], axis=1)
    d_normed += dot_t(d_left_pre.astype(jnp.bfloat16), w_left_ref[...])

    each(0, n_row, lambda slot: arrived(grad_col, grad_col_in, slot))
    grad_col_wide[...] = grad_col[...].astype(jnp.float32)

    def add_right(source, sums):
        sums = list(sums)
        left = panel[source, 0].astype(jnp.float32)
        for i in range(rows):
            left_i = left[i * cols : (i + 1) * cols]
            for j in range(rows):
                sums[j] += grad_col_wide[source, i * rows + j : i * rows + j + 1, :] * left_i
        return tuple(sums)

    d_right = jnp.concatenate(loop(n_row, add_right, (zero_wide,) * rows), axis=0)
    right_part = d_right * pair_mask * right_sig
    d_right_pre = jnp.concatenate([right_part, right_part * right_lin * (1.0 - right_sig)], axis=1)
    d_normed += dot_t(d_right_pre.astype(jnp.bfloat16), w_right_ref[...])
    out_ref[...] = norm_back(d_normed * gain_in, hat_in, inv_in).astype(jnp.bfloat16)

    each(1, n_row, lambda step: turn_copy(step).wait_send())

    @pl.when(home_col != col)
    def _():
        turn_copy(0).wait_send()

    each(1, n_col, lambda step: left_row_copy(step).wait_send())
    each(1, n_row, lambda step: panel_copy(step).wait_send())
    each(1, n_col, lambda step: grad_row_copy(step).wait_send())
    for part in range(ratio):

        def sent_part(to_col, part=part):
            own = jnp.logical_and(col * ratio + part == row, to_col == col)

            @pl.when(jnp.logical_not(own))
            def _():
                grad_col_copy(part, to_col).wait_send()

        each(0, n_col, sent_part)


def solution(mesh):
    n_row = mesh.shape["row"]
    n_col = mesh.shape["col"]

    def shards(
        pair_act,
        cotangent,
        crop_len,
        ln_in_gain,
        ln_in_bias,
        w_left,
        w_right,
        w_gate,
        ln_out_gain,
        ln_out_bias,
        w_out,
    ):
        rows, cols, channels = pair_act.shape
        width = w_out.shape[0]
        ratio = cols // rows
        assert ratio * rows == cols and n_row * rows == n_col * cols
        cells, sub = rows * cols, rows * rows
        half, full, sems = jnp.bfloat16, jnp.float32, pltpu.SemaphoreType.DMA
        result = pl.pallas_call(
            functools.partial(kernel, n_row, n_col, rows, cols),
            out_shape=pltpu.VMEM((cells, channels), half),
            in_specs=[pl.BlockSpec(memory_space=pltpu.HBM)] * 11,
            out_specs=pl.BlockSpec(memory_space=pltpu.VMEM),
            scratch_shapes=[
                pltpu.SMEM(crop_len.shape, jnp.int32),
                pltpu.VMEM((cells, channels), half),
                pltpu.VMEM((cells, channels), half),
                pltpu.VMEM((1, channels), full),
                pltpu.VMEM((1, channels), full),
                pltpu.VMEM(w_left.shape, half),
                pltpu.VMEM(w_right.shape, half),
                pltpu.VMEM(w_gate.shape, half),
                pltpu.VMEM((1, width), full),
                pltpu.VMEM((1, width), full),
                pltpu.VMEM(w_out.shape, half),
                sems((11,)),
                pltpu.VMEM((2, cells, width), half),
                pltpu.VMEM((cells, width), half),
                pltpu.VMEM((ratio, sub, width), half),
                pltpu.VMEM((n_col, cells, width), half),
                pltpu.VMEM((ratio * n_col, cells, width), half),
                pltpu.VMEM((n_row, 2, cells, width), half),
                pltpu.VMEM((n_row, sub, width), half),
                pltpu.VMEM((n_row, sub, width), half),
                pltpu.VMEM((cells, width), full),
                pltpu.VMEM((n_col, cells, width), full),
                pltpu.VMEM((n_row, sub, width), full),
                pltpu.VMEM((n_row, sub, width), full),
                sems((n_col,)),
                sems((n_col,)),
                sems((n_row,)),
                sems((ratio * n_col,)),
                sems((n_row,)),
                sems((n_row,)),
                sems((n_col,)),
                sems((n_col,)),
                sems((ratio * n_col,)),
                sems((n_row,)),
            ],
            compiler_params=pltpu.CompilerParams(
                collective_id=0, has_side_effects=True, vmem_limit_bytes=60 * 1024 * 1024
            ),
        )(
            crop_len,
            pair_act.reshape(cells, channels),
            cotangent.reshape(cells, channels),
            ln_in_gain.reshape(1, channels),
            ln_in_bias.reshape(1, channels),
            w_left,
            w_right,
            w_gate,
            ln_out_gain.reshape(1, width),
            ln_out_bias.reshape(1, width),
            w_out,
        )
        return result.reshape(rows, cols, channels)

    pair_spec = P(("groups", "row"), "col", None)
    return jax.shard_map(
        shards,
        mesh=mesh,
        in_specs=(pair_spec, pair_spec, P("groups")) + (P(),) * 8,
        out_specs=pair_spec,
        check_vma=False,
    )
```

```python
import functools

import jax
import jax.numpy as jnp
from jax import lax
from jax.experimental import pallas as pl
from jax.experimental.pallas import tpu as pltpu
from jax.sharding import PartitionSpec as P

epsilon = 1e-05
MESH = pl.DeviceIdType.MESH


def normalize(values):
    center = jnp.mean(values, axis=-1, keepdims=True)
    shifted = values - center
    inv_std = lax.rsqrt(jnp.mean(shifted * shifted, axis=-1, keepdims=True) + epsilon)
    return (shifted * inv_std, inv_std)


def norm_back(d_scaled, scaled, inv_std):
    first = jnp.mean(d_scaled, axis=-1, keepdims=True)
    second = jnp.mean(d_scaled * scaled, axis=-1, keepdims=True)
    return inv_std * (d_scaled - first - scaled * second)


def dot(a, b):
    return jnp.dot(a, b, preferred_element_type=jnp.float32)


def dot_t(a, b):
    return lax.dot_general(a, b, (((1,), (1,)), ((), ())), preferred_element_type=jnp.float32)


def loop(count, body, init):
    if count <= 4:
        for step in range(count):
            init = body(step, init)
        return init
    return lax.fori_loop(0, count, body, init)


def each(start, count, body):
    if count <= 16:
        for step in range(start, count):
            body(step)
    else:

        @pl.loop(start, count)
        def _(step):
            body(step)


def kernel(
    n_row,
    n_col,
    rows,
    cols,
    crop_hbm,
    pair_hbm,
    cot_hbm,
    gain_in_hbm,
    bias_in_hbm,
    w_left_hbm,
    w_right_hbm,
    w_gate_hbm,
    gain_out_hbm,
    bias_out_hbm,
    w_out_hbm,
    out_ref,
    crop_ref,
    pair_ref,
    cot_ref,
    gain_in_ref,
    bias_in_ref,
    w_left_ref,
    w_right_ref,
    w_gate_ref,
    gain_out_ref,
    bias_out_ref,
    w_out_ref,
    load_in,
    side_own,
    turn_own,
    grad_own,
    left_row,
    right_turn,
    panel,
    grad_row,
    grad_col,
    right_wide,
    left_wide,
    grad_row_wide,
    grad_col_wide,
    left_row_out,
    left_row_in,
    turn_out,
    turn_in,
    panel_out,
    panel_in,
    grad_row_out,
    grad_row_in,
    grad_col_out,
    grad_col_in,
):
    row = lax.axis_index("row")
    col = lax.axis_index("col")
    ratio = cols // rows
    cells = rows * cols
    sub = rows * rows
    width = w_out_ref.shape[0]
    home_col = row // ratio
    total = n_row * n_col

    barrier = pltpu.get_barrier_semaphore()

    pairs = (
        (pair_hbm, pair_ref),
        (gain_in_hbm, gain_in_ref),
        (bias_in_hbm, bias_in_ref),
        (w_right_hbm, w_right_ref),
        (crop_hbm, crop_ref),
        (w_left_hbm, w_left_ref),
        (w_gate_hbm, w_gate_ref),
        (cot_hbm, cot_ref),
        (w_out_hbm, w_out_ref),
        (gain_out_hbm, gain_out_ref),
        (bias_out_hbm, bias_out_ref),
    )
    loads = [pltpu.make_async_copy(*pair, load_in.at[at]) for at, pair in enumerate(pairs)]
    for load in loads[:5]:
        load.start()

    def greet(step):
        other = lax.rem(row * n_col + col + step, total)
        other_row, other_col = other // n_col, lax.rem(other, n_col)
        same_row = jnp.logical_or(other_row == row, other_row // ratio == col)
        same_col = jnp.logical_or(other_col == col, other_col == home_col)

        @pl.when(jnp.logical_or(same_row, same_col))
        def _():
            pl.semaphore_signal(
                barrier,
                inc=1,
                device_id={"row": other_row, "col": other_col},
                device_id_type=MESH,
            )

    each(1, total, greet)
    apart = (home_col != col).astype(jnp.int32)
    row_count, col_count = ratio + apart, 1 + apart
    greeted = row_count * n_col + col_count * n_row - row_count * col_count - 1
    for load in loads[5:]:
        load.start()

    def remote(src, dst, out_sem, in_sem, to_row, to_col):
        return pltpu.make_async_remote_copy(
            src_ref=src,
            dst_ref=dst,
            send_sem=out_sem,
            recv_sem=in_sem,
            device_id={"row": to_row, "col": to_col},
            device_id_type=MESH,
        )

    for load in loads[:5]:
        load.wait()
    position = (rows, cols, width)
    row_pos = row * rows + lax.broadcasted_iota(jnp.int32, position, 0)
    col_pos = col * cols + lax.broadcasted_iota(jnp.int32, position, 1)
    crop = crop_ref[0]
    pair_mask = jnp.where(jnp.maximum(row_pos, col_pos) < crop, 1.0, 0.0).reshape(cells, width)
    hat_in, inv_in = normalize(pair_ref[...].astype(jnp.float32))
    gain_in = gain_in_ref[...]
    normed = (hat_in * gain_in + bias_in_ref[...]).astype(jnp.bfloat16)
    right_proj = dot(normed, w_right_ref[...])
    right_lin = right_proj[:, :width]
    right_sig = jax.nn.sigmoid(right_proj[:, width:])
    right_side = (pair_mask * right_sig * right_lin).astype(jnp.bfloat16)
    side_own[1] = right_side
    right_wide[...] = right_side.astype(jnp.float32)
    turn_own[...] = jnp.concatenate(
        [right_wide[pl.ds(k, rows, stride=cols), :] for k in range(cols)], axis=0
    ).astype(jnp.bfloat16)

    pl.semaphore_wait(barrier, greeted)

    turn_slot = lax.rem(row, ratio) * n_col + col

    def turn_copy(step):
        return remote(
            turn_own,
            right_turn.at[turn_slot],
            turn_out.at[step],
            turn_in.at[turn_slot],
            lax.rem(row + step, n_row),
            home_col,
        )

    each(1, n_row, lambda step: turn_copy(step).start())

    @pl.when(home_col != col)
    def _():
        turn_copy(0).start()

    @pl.when(home_col == col)
    def _():
        pltpu.make_async_copy(turn_own, right_turn.at[turn_slot], turn_in.at[turn_slot]).start()

    loads[5].wait()
    left_proj = dot(normed, w_left_ref[...])
    left_lin = left_proj[:, :width]
    left_sig = jax.nn.sigmoid(left_proj[:, width:])
    side_own[0] = (pair_mask * left_sig * left_lin).astype(jnp.bfloat16)

    def left_row_copy(step):
        return remote(
            side_own.at[0],
            left_row.at[col],
            left_row_out.at[step],
            left_row_in.at[col],
            row,
            lax.rem(col + step, n_col),
        )

    each(1, n_col, lambda step: left_row_copy(step).start())

    def panel_copy(step):
        return remote(
            side_own,
            panel.at[row],
            panel_out.at[step],
            panel_in.at[row],
            lax.rem(row + step, n_row),
            col,
        )

    each(1, n_row, lambda step: panel_copy(step).start())

    left_row[col] = side_own[0]
    panel[row] = side_own[...]

    for load in loads[6:]:
        load.wait()
    gating = jax.nn.sigmoid(dot(normed, w_gate_ref[...]))
    cot_full = cot_ref[...].astype(jnp.float32)
    d_proj = (cot_full * gating).astype(jnp.bfloat16)
    gain_out = gain_out_ref[...]
    d_scaled = dot_t(d_proj, w_out_ref[...]) * gain_out

    def arrived(buffer, sem, slot):
        remote(buffer.at[slot], buffer.at[slot], sem.at[slot], sem.at[slot], row, col).wait_recv()

    each(1, n_col, lambda step: arrived(left_row, left_row_in, lax.rem(col + step, n_col)))
    each(0, ratio * n_col, lambda slot: arrived(right_turn, turn_in, slot))

    left_wide[...] = left_row[...].astype(jnp.float32)

    def add_update(source, sums):
        sums = list(sums)
        for part in range(ratio):
            turned = right_turn[part * n_col + source].astype(jnp.float32)
            for k in range(cols):
                turned_k = turned[k * rows : (k + 1) * rows]
                for i in range(rows):
                    at = part * rows + i
                    sums[at] += left_wide[source, i * cols + k : i * cols + k + 1, :] * turned_k
        return tuple(sums)

    zero = jnp.zeros((rows, width), jnp.float32)
    sums = loop(n_col, add_update, (zero,) * (ratio * rows))
    update = jnp.concatenate(
        [sums[part * rows + i] for i in range(rows) for part in range(ratio)], axis=0
    )
    hat_out, inv_out = normalize(update)
    d_update = norm_back(d_scaled, hat_out, inv_out)
    for part in range(ratio):
        grad_own[part] = jnp.concatenate(
            [
                d_update[i * cols + part * rows : i * cols + (part + 1) * rows]
                for i in range(rows)
            ],
            axis=0,
        ).astype(jnp.bfloat16)

    def grad_col_copy(part, to_col):
        return remote(
            grad_own.at[part],
            grad_col.at[row],
            grad_col_out.at[part * n_col + to_col],
            grad_col_in.at[row],
            col * ratio + part,
            to_col,
        )

    for part in range(ratio):

        def send_part(to_col, part=part):
            own = jnp.logical_and(col * ratio + part == row, to_col == col)

            @pl.when(jnp.logical_not(own))
            def _():
                grad_col_copy(part, to_col).start()

            @pl.when(own)
            def _():
                pltpu.make_async_copy(
                    grad_own.at[part], grad_col.at[row], grad_col_in.at[row]
                ).start()

        each(0, n_col, send_part)

    def grad_row_copy(step):
        slots = pl.ds(col * ratio, ratio)
        return remote(
            grad_own,
            grad_row.at[slots],
            grad_row_out.at[step],
            grad_row_in.at[col],
            row,
            lax.rem(col + step, n_col),
        )

    each(1, n_col, lambda step: grad_row_copy(step).start())
    grad_row[pl.ds(col * ratio, ratio)] = grad_own[...]

    mixed = (hat_out * gain_out + bias_out_ref[...]).astype(jnp.bfloat16)
    proj_out = dot(mixed, w_out_ref[...])
    d_gate_pre = (cot_full * proj_out * gating * (1.0 - gating)).astype(jnp.bfloat16)
    d_normed = dot_t(d_gate_pre, w_gate_ref[...])
    each(1, n_row, lambda step: arrived(panel, panel_in, lax.rem(row + step, n_row)))

    def grad_row_arrived(step):
        source = lax.rem(col + step, n_col)
        slots = pl.ds(source * ratio, ratio)
        remote(
            grad_row.at[slots],
            grad_row.at[slots],
            grad_row_in.at[source],
            grad_row_in.at[source],
            row,
            col,
        ).wait_recv()

    each(1, n_col, grad_row_arrived)
    grad_row_wide[...] = grad_row[...].astype(jnp.float32)

    def add_left(source, sums):
        sums = list(sums)
        right = panel[source, 1].astype(jnp.float32)
        for j in range(rows):
            right_j = right[j * cols : (j + 1) * cols]
            for i in range(rows):
                sums[i] += grad_row_wide[source, i * rows + j : i * rows + j + 1, :] * right_j
        return tuple(sums)

    zero_wide = jnp.zeros((cols, width), jnp.float32)
    d_left = jnp.concatenate(loop(n_row, add_left, (zero_wide,) * rows), axis=0)
    left_part = d_left * pair_mask * left_sig
    d_left_pre = jnp.concatenate([left_part, left_part * left_lin * (1.0 - left_sig)], axis=1)
    d_normed += dot_t(d_left_pre.astype(jnp.bfloat16), w_left_ref[...])

    each(0, n_row, lambda slot: arrived(grad_col, grad_col_in, slot))
    grad_col_wide[...] = grad_col[...].astype(jnp.float32)

    def add_right(source, sums):
        sums = list(sums)
        left = panel[source, 0].astype(jnp.float32)
        for i in range(rows):
            left_i = left[i * cols : (i + 1) * cols]
            for j in range(rows):
                sums[j] += grad_col_wide[source, i * rows + j : i * rows + j + 1, :] * left_i
        return tuple(sums)

    d_right = jnp.concatenate(loop(n_row, add_right, (zero_wide,) * rows), axis=0)
    right_part = d_right * pair_mask * right_sig
    d_right_pre = jnp.concatenate([right_part, right_part * right_lin * (1.0 - right_sig)], axis=1)
    d_normed += dot_t(d_right_pre.astype(jnp.bfloat16), w_right_ref[...])
    out_ref[...] = norm_back(d_normed * gain_in, hat_in, inv_in).astype(jnp.bfloat16)

    each(1, n_row, lambda step: turn_copy(step).wait_send())

    @pl.when(home_col != col)
    def _():
        turn_copy(0).wait_send()

    each(1, n_col, lambda step: left_row_copy(step).wait_send())
    each(1, n_row, lambda step: panel_copy(step).wait_send())
    each(1, n_col, lambda step: grad_row_copy(step).wait_send())
    for part in range(ratio):

        def sent_part(to_col, part=part):
            own = jnp.logical_and(col * ratio + part == row, to_col == col)

            @pl.when(jnp.logical_not(own))
            def _():
                grad_col_copy(part, to_col).wait_send()

        each(0, n_col, sent_part)


def solution(mesh):
    n_row = mesh.shape["row"]
    n_col = mesh.shape["col"]

    def shards(
        pair_act,
        cotangent,
        crop_len,
        ln_in_gain,
        ln_in_bias,
        w_left,
        w_right,
        w_gate,
        ln_out_gain,
        ln_out_bias,
        w_out,
    ):
        rows, cols, channels = pair_act.shape
        width = w_out.shape[0]
        ratio = cols // rows
        assert ratio * rows == cols and n_row * rows == n_col * cols
        cells, sub = rows * cols, rows * rows
        half, full, sems = jnp.bfloat16, jnp.float32, pltpu.SemaphoreType.DMA
        result = pl.pallas_call(
            functools.partial(kernel, n_row, n_col, rows, cols),
            out_shape=pltpu.VMEM((cells, channels), half),
            in_specs=[pl.BlockSpec(memory_space=pltpu.HBM)] * 11,
            out_specs=pl.BlockSpec(memory_space=pltpu.VMEM),
            scratch_shapes=[
                pltpu.SMEM(crop_len.shape, jnp.int32),
                pltpu.VMEM((cells, channels), half),
                pltpu.VMEM((cells, channels), half),
                pltpu.VMEM((1, channels), full),
                pltpu.VMEM((1, channels), full),
                pltpu.VMEM(w_left.shape, half),
                pltpu.VMEM(w_right.shape, half),
                pltpu.VMEM(w_gate.shape, half),
                pltpu.VMEM((1, width), full),
                pltpu.VMEM((1, width), full),
                pltpu.VMEM(w_out.shape, half),
                sems((11,)),
                pltpu.VMEM((2, cells, width), half),
                pltpu.VMEM((cells, width), half),
                pltpu.VMEM((ratio, sub, width), half),
                pltpu.VMEM((n_col, cells, width), half),
                pltpu.VMEM((ratio * n_col, cells, width), half),
                pltpu.VMEM((n_row, 2, cells, width), half),
                pltpu.VMEM((n_row, sub, width), half),
                pltpu.VMEM((n_row, sub, width), half),
                pltpu.VMEM((cells, width), full),
                pltpu.VMEM((n_col, cells, width), full),
                pltpu.VMEM((n_row, sub, width), full),
                pltpu.VMEM((n_row, sub, width), full),
                sems((n_col,)),
                sems((n_col,)),
                sems((n_row,)),
                sems((ratio * n_col,)),
                sems((n_row,)),
                sems((n_row,)),
                sems((n_col,)),
                sems((n_col,)),
                sems((ratio * n_col,)),
                sems((n_row,)),
            ],
            compiler_params=pltpu.CompilerParams(
                collective_id=0, has_side_effects=True, vmem_limit_bytes=60 * 1024 * 1024
            ),
        )(
            crop_len,
            pair_act.reshape(cells, channels),
            cotangent.reshape(cells, channels),
            ln_in_gain.reshape(1, channels),
            ln_in_bias.reshape(1, channels),
            w_left,
            w_right,
            w_gate,
            ln_out_gain.reshape(1, width),
            ln_out_bias.reshape(1, width),
            w_out,
        )
        return result.reshape(rows, cols, channels)

    pair_spec = P(("groups", "row"), "col", None)
    return jax.shard_map(
        shards,
        mesh=mesh,
        in_specs=(pair_spec, pair_spec, P("groups")) + (P(),) * 8,
        out_specs=pair_spec,
        check_vma=False,
    )
```
